512 devices in a mesh: store: 32 (over z, y_lo, core), prod: 16 (over y_hi, x).
Axes of the slice: x: 4, y: 8 (y_hi: 4, y_lo: 2; y = y_hi * 2 + y_lo), z: 8, core: 2. Of those that a mesh axis runs over, the one named last changes fastest.
Arguments:
- gradients: bfloat16 [196608, 2048], P(('store', 'prod')), may hold values from -6 to 6
- destinations: int32 [196608], P(('store', 'prod')), may hold values from 0 to 31, as said below
- queries: bfloat16 [1536, 2048], P(('store', 'prod')), may hold values from -6 to 6
- left_factor: float32 [32, 32], replicated, may hold values from -11 to 11, as said below
- right_factor: float32 [64, 64], replicated, may hold values from -11 to 11, as said below
Outputs:
- scores: bfloat16 [1536, 393216], P(None, ('store', 'prod'))
The draws below stay inside these ranges and needn't reach their ends.
Inputs may be any that keep to these rules, and one draw needn't show every extreme that they name: `destinations`: within the rows of one producer (aligned blocks of 384 rows) no store index is named more than 24 times, and one store index, the same for every producer, is named exactly 24 times in every block. `left_factor`: a dense real matrix. `right_factor`: a dense real matrix.
All inputs are finite; a program needn't handle non-finite values.
Results may differ from the reference program's by a relative error of at most 0.0049.
Values may be sent and summed in bfloat16 or wider, within the bound.
No kernel may reach another device: no remote copies, remote signals or barrier semaphores. Data moves between devices by JAX's collectives and lax.ppermute only.
A program may use at most 64 MiB of HBM per device.

```python
import math
import jax
import jax.numpy as jnp
from jax import lax

FA = 32
FB = 64
D = 2048
ROWS_DEV = 384
OWNERS = 32
LANES = 16
MOST = 24
CAP = 768
ROWS = 196608
QUERIES = 1536
SLOTS = 393216
DEVICES = 512


def scaled_factor(key, dimension, along_rows):
    entry_key = jax.random.fold_in(key, 11)
    scale_key = jax.random.fold_in(key, 13)
    entries = jnp.clip(jax.random.normal(entry_key, (dimension, dimension), jnp.float32), -6.0, 6.0)
    spread = jnp.exp(jax.random.uniform(scale_key, (dimension,), jnp.float32, 0.0, math.log(10.0)))
    entries = entries / math.sqrt(dimension)
    if along_rows:
        scaled = entries * spread[:, None]
    else:
        scaled = entries * spread[None, :]
    return jnp.clip(scaled, -10.0, 10.0)


def draw_left_factor(key, part):
    return scaled_factor(key, FA, True)


def draw_right_factor(key, part):
    return scaled_factor(key, FB, False)


def draw_destinations(key, part):
    hottest = jax.random.randint(jax.random.fold_in(key, 3), (), 0, OWNERS).astype(jnp.int32)
    others = OWNERS - 1

    def one_block(block_key):
        chosen = jax.random.permutation(block_key, others * MOST)[:ROWS_DEV - MOST].astype(jnp.int32)
        spare = chosen // MOST
        spare = spare + (spare >= hottest).astype(jnp.int32)
        merged = jnp.concatenate([jnp.full((MOST,), hottest, jnp.int32), spare.astype(jnp.int32)])
        return jax.random.permutation(jax.random.fold_in(block_key, 5), merged)
    block_keys = jax.random.split(jax.random.fold_in(key, 4), ROWS // ROWS_DEV)
    return jax.vmap(one_block)(block_keys).reshape((ROWS,)).astype(jnp.int32)


def steps_of(own_key, dims, shards, low, largest):
    loudness, own = 1.0, jax.random.fold_in(own_key, 6)
    for position, shards_of in shards:
        heights = jnp.exp(jax.random.uniform(jax.random.fold_in(own, position), (shards_of,), jnp.float32, low / len(shards), largest / len(shards)))
        loudness = loudness * jnp.repeat(heights, dims[position] // shards_of).reshape([-1 if axis == position else 1 for axis in range(len(dims))])
    return loudness


def noise(rng, extent, scale, bound, cuts=(), kind=jnp.bfloat16):
    values = scale * jax.random.normal(rng, extent, jnp.float32)
    if cuts:
        values = values * steps_of(rng, extent, cuts, -0.22, 0.18)
    return jnp.clip(values, -bound, bound).astype(kind)


def setup_inputs(seed: int = 0) -> dict:
    keys = jax.random.split(jax.random.key(seed), 6)
    gradients = noise(keys[0], (ROWS, D), 1.0, 6.0, ((0, 512),))
    destinations = draw_destinations(jax.random.fold_in(keys[5], 71), 0)
    queries = noise(keys[2], (QUERIES, D), 1.0, 6.0, ((0, 512),))
    left_factor = draw_left_factor(jax.random.fold_in(keys[5], 71), 0)
    right_factor = draw_right_factor(jax.random.fold_in(keys[5], 71), 0)
    return dict(gradients=gradients, destinations=destinations, queries=queries, left_factor=left_factor, right_factor=right_factor)


def precondition(gradients, left_factor, right_factor):
    leading = gradients.shape[:-1]
    matrices = gradients.astype(jnp.float32).reshape((-1, FA, FB))
    right_done = jnp.einsum('nbc,cd->nbd', matrices, right_factor.astype(jnp.float32), precision=lax.Precision.HIGHEST)
    product = jnp.einsum('ab,nbd->nad', left_factor.astype(jnp.float32), right_done, precision=lax.Precision.HIGHEST)
    product = product.reshape(leading + (FA * FB,))
    scaling = lax.rsqrt(lax.optimization_barrier(jnp.mean(product * product, axis=-1, keepdims=True)) + 1e-06)
    return (product * scaling * (1.0 / math.sqrt(FA * FB))).astype(jnp.bfloat16)

def row_ranks(targets, owners):
    matches = (targets[:, None] == jnp.arange(owners, dtype=jnp.int32)[None, :]).astype(jnp.int32)
    earlier = jnp.cumsum(matches, axis=0) - matches
    return lax.optimization_barrier(jnp.sum(earlier * matches, axis=1)).astype(jnp.int32)

def reference(gradients, destinations, queries, left_factor, right_factor):
    grad_blocks = gradients.reshape((DEVICES, ROWS_DEV, D))
    target_blocks = destinations.reshape((DEVICES, ROWS_DEV))

    def absorb(scores, packed):
        producer, row_block, targets = packed
        normal = precondition(row_block, left_factor, right_factor)
        column = jnp.dot(queries, normal.T, preferred_element_type=jnp.float32).astype(jnp.bfloat16)
        source = producer // LANES
        lane_index = producer % LANES
        places = (targets * LANES + lane_index) * CAP + source * MOST + row_ranks(targets, OWNERS)
        return (scores.at[:, places].set(column), None)
    initial = jnp.zeros((QUERIES, SLOTS), jnp.bfloat16)
    scores, unused = lax.scan(absorb, initial, (jnp.arange(DEVICES, dtype=jnp.int32), grad_blocks, target_blocks))
    return scores
```

```python
import math

import jax
import jax.numpy as jnp
from jax import lax
from jax.experimental import pallas as pl
from jax.experimental.pallas import tpu as pltpu
from jax.sharding import Mesh, PartitionSpec as P

STORE = ("z", "y_lo", "core")
PROD = ("y_hi", "x")
HIGHEST = lax.Precision.HIGHEST


def exchange(block, axis):
    return lax.all_to_all(block, axis, split_axis=0, concat_axis=0, tiled=True)


def gather(block, axis):
    count = lax.axis_size(axis)
    return exchange(jnp.broadcast_to(block[None], (count,) + block.shape), axis)


def kron(left, matrices, right):
    rows = matrices.shape[0]
    cubes = matrices.astype(jnp.float32).reshape((rows, left.shape[1], right.shape[0]))
    half = jnp.einsum("nbc,cd->nbd", cubes, right, precision=HIGHEST)
    return jnp.einsum("ab,nbd->nad", left, half, precision=HIGHEST)


def slots_of(targets, bucket):
    rows = targets.shape[1]
    above = lax.broadcasted_iota(jnp.int32, (rows, rows), 0)
    along = lax.broadcasted_iota(jnp.int32, (rows, rows), 1)
    upright = jnp.sum(jnp.where(above == along, targets, 0), axis=1, keepdims=True)
    earlier = jnp.where((upright == targets) & (above < along), 1, 0)
    return targets * bucket + jnp.sum(earlier, axis=0, keepdims=True)


def place(gradients, targets, bucket, capacity):
    rows, width = gradients.shape
    step = 512

    def kernel(targets_ref, rows_ref, out_ref, slots_ref, pick):
        @pl.when(pl.program_id(0) == 0)
        def _():
            slots = slots_of(targets_ref[...], bucket)
            slots_ref[...] = slots
            at = lax.broadcasted_iota(jnp.int32, (capacity, rows), 0)
            pick[...] = jnp.where(at == slots, 1.0, 0.0).astype(jnp.bfloat16)

        out_ref[...] = jnp.dot(
            pick[...], rows_ref[...], preferred_element_type=jnp.float32
        ).astype(jnp.bfloat16)

    return pl.pallas_call(
        kernel,
        grid=(width // step,),
        in_specs=[
            pl.BlockSpec((1, rows), lambda i: (0, 0)),
            pl.BlockSpec((rows, step), lambda i: (0, i)),
        ],
        out_specs=[
            pl.BlockSpec((capacity, step), lambda i: (0, i)),
            pl.BlockSpec((1, rows), lambda i: (0, 0)),
        ],
        out_shape=[
            jax.ShapeDtypeStruct((capacity, width), jnp.bfloat16),
            jax.ShapeDtypeStruct((1, rows), jnp.int32),
        ],
        scratch_shapes=[pltpu.VMEM((capacity, rows), jnp.bfloat16)],
        compiler_params=pltpu.CompilerParams(vmem_limit_bytes=24 * 2**20),
        cost_estimate=pl.CostEstimate(
            flops=2 * capacity * rows * width, bytes_accessed=5 * 2**20, transcendentals=0
        ),
    )(targets, gradients)


def precondition(gradients, left, right):
    product = kron(left, gradients, right).reshape(gradients.shape)
    scale = lax.rsqrt(jnp.mean(product * product, axis=-1, keepdims=True) + 1e-06)
    return (product * scale * (1.0 / math.sqrt(product.shape[1]))).astype(jnp.bfloat16)


def reorder(blocks, order):
    outer, pairs, rows, width = blocks.shape
    deep, high, own = order
    inner = rows // deep * outer

    def kernel(in_ref, out_ref):
        total = outer * rows
        to = lax.broadcasted_iota(jnp.int32, (total, total), 0)
        source = lax.broadcasted_iota(jnp.int32, (total, total), 1)
        at_x = source // rows
        at_z = source % rows // (high * own)
        at_high = source % (high * own) // own
        goes = at_z * inner + (at_high * outer + at_x) * own + source % own
        pick = jnp.where(to == goes, 1.0, 0.0).astype(jnp.bfloat16)
        moved = jnp.dot(
            pick, in_ref[...].reshape((total, width)), preferred_element_type=jnp.float32
        )
        out_ref[...] = moved.astype(jnp.bfloat16).reshape((deep, 1, inner, width))

    return pl.pallas_call(
        kernel,
        grid=(pairs,),
        in_specs=[pl.BlockSpec((outer, 1, rows, width), lambda i: (0, i, 0, 0))],
        out_specs=pl.BlockSpec((deep, 1, inner, width), lambda i: (0, i, 0, 0)),
        out_shape=jax.ShapeDtypeStruct((deep, pairs, inner, width), jnp.bfloat16),
        compiler_params=pltpu.CompilerParams(vmem_limit_bytes=32 * 2**20),
        cost_estimate=pl.CostEstimate(
            flops=2 * pairs * (outer * rows) ** 2 * width,
            bytes_accessed=4 * pairs * outer * rows * width,
            transcendentals=0,
        ),
    )(blocks)


def body(gradients, destinations, queries, left_factor, right_factor):
    sizes = {axis: lax.axis_size(axis) for axis in STORE + PROD}
    owners = lax.axis_size(STORE)
    rows, width = gradients.shape
    bucket = 2 * rows // owners
    capacity = owners * bucket
    own = queries.shape[0]

    few = gather(queries, ("z", "y_hi")).reshape((-1, width))
    normal = precondition(gradients, left_factor, right_factor)
    buffer, slots = place(normal, destinations[None], bucket, capacity)
    few, buffer = lax.optimization_barrier((few, buffer))

    every = lax.all_gather(few, ("x", "y_lo", "core"), axis=0, tiled=True)
    every = every.reshape((sizes["x"], -1, few.shape[0], width))
    every = reorder(every, (sizes["z"], sizes["y_hi"], own)).reshape((-1, width))

    stored = exchange(buffer.reshape((owners, bucket, width)), STORE).reshape((capacity, width))
    scores = lax.dot_general(
        every, stored, (((1,), (1,)), ((), ())), preferred_element_type=jnp.float32
    )
    return scores.astype(jnp.bfloat16)


def solution(mesh):
    fine = Mesh(mesh.devices.reshape((8, 2, 2, 4, 4)), STORE + PROD)
    whole = STORE + PROD
    return jax.shard_map(
        body,
        mesh=fine,
        in_specs=(P(whole, None), P(whole), P(whole, None), P(), P()),
        out_specs=P(None, whole),
        check_vma=False,
    )
```

```python
import math

import jax
import jax.numpy as jnp
from jax import lax
from jax.experimental import pallas as pl
from jax.experimental.pallas import tpu as pltpu
from jax.sharding import Mesh, PartitionSpec as P

STORE = ("z", "y_lo", "core")
PROD = ("y_hi", "x")
VMEM = pl.BlockSpec(memory_space=pltpu.VMEM)


def exchange(block, axis):
    return lax.all_to_all(block, axis, split_axis=0, concat_axis=0, tiled=True)


def gather(block, axis):
    count = lax.axis_size(axis)
    return exchange(jnp.broadcast_to(block[None], (count,) + block.shape), axis)


def shift(block, axis, by):
    count = lax.axis_size(axis)
    return lax.ppermute(block, axis, [(i, (i + by) % count) for i in range(count)])


def slots_of(targets, bucket):
    rows = targets.shape[1]
    above = lax.broadcasted_iota(jnp.int32, (rows, rows), 0)
    along = lax.broadcasted_iota(jnp.int32, (rows, rows), 1)
    upright = jnp.sum(jnp.where(above == along, targets, 0), axis=1, keepdims=True)
    earlier = jnp.where((upright == targets) & (above < along), 1, 0)
    return targets * bucket + jnp.sum(earlier, axis=0, keepdims=True)


def prepare(gradients, targets, left, right, bucket, capacity, step=512):
    rows, width = gradients.shape
    deep, fine = left.shape[1], right.shape[0]
    steps = width // step
    spread = jnp.repeat(left.T, fine, axis=1)
    tiled = jnp.tile(right, (1, step // fine))

    def kernel(targets_ref, rows_ref, spread_ref, tiled_ref, out_ref, product, squares, pick):
        i = pl.program_id(0)

        @pl.when(i == 0)
        def _():
            squares[...] = jnp.zeros_like(squares)

        @pl.when(i < steps)
        def _():
            factor = spread_ref[...][:, None, :] * tiled_ref[...][None]
            factor = factor.reshape((width, step))
            high = factor.astype(jnp.bfloat16)
            low = (factor - high.astype(jnp.float32)).astype(jnp.bfloat16)
            part = jnp.dot(rows_ref[...], high, preferred_element_type=jnp.float32)
            part = part + jnp.dot(rows_ref[...], low, preferred_element_type=jnp.float32)
            product[i] = part
            squares[...] += jnp.sum(part * part, axis=1, keepdims=True)

        @pl.when(i == steps)
        def _():
            slots = slots_of(targets_ref[...], bucket)
            at = lax.broadcasted_iota(jnp.int32, (capacity, rows), 0)
            pick[...] = jnp.where(at == slots, 1.0, 0.0).astype(jnp.bfloat16)
            squares[...] = lax.rsqrt(squares[...] / width + 1e-06) * (1.0 / math.sqrt(width))

        @pl.when(i >= steps)
        def _():
            normal = (product[i - steps] * squares[...]).astype(jnp.bfloat16)
            out_ref[...] = jnp.dot(
                pick[...], normal, preferred_element_type=jnp.float32
            ).astype(jnp.bfloat16)

    return pl.pallas_call(
        kernel,
        grid=(2 * steps,),
        in_specs=[
            pl.BlockSpec((1, rows), lambda i: (0, 0)),
            pl.BlockSpec((rows, width), lambda i: (0, 0)),
            pl.BlockSpec((deep, step), lambda i: (0, jnp.minimum(i, steps - 1))),
            pl.BlockSpec((fine, step), lambda i: (0, 0)),
        ],
        out_specs=pl.BlockSpec((capacity, step), lambda i: (0, jnp.maximum(i - steps, 0))),
        out_shape=jax.ShapeDtypeStruct((capacity, width), jnp.bfloat16),
        scratch_shapes=[
            pltpu.VMEM((steps, rows, step), jnp.float32),
            pltpu.VMEM((rows, 1), jnp.float32),
            pltpu.VMEM((capacity, rows), jnp.bfloat16),
        ],
        compiler_params=pltpu.CompilerParams(vmem_limit_bytes=60 * 2**20),
        cost_estimate=pl.CostEstimate(
            flops=2 * rows * width * (2 * width + capacity),
            bytes_accessed=6 * 2**20,
            transcendentals=0,
        ),
    )(targets, gradients, spread, tiled)


def reorder(place_of, pair, before, after, far, order):
    deep, high, own = order
    flips, rows, width = pair.shape
    outer = lax.axis_size("x")
    inner = high * outer * own
    total = outer * rows

    def kernel(at_ref, pair_ref, before_ref, after_ref, far0_ref, far1_ref, out_ref, held, sems):
        copies = []
        for flip, far_ref in enumerate((far0_ref, far1_ref)):
            sources = [ref.at[flip] for ref in (pair_ref, before_ref, after_ref)] + [far_ref]
            for s, source_ref in enumerate(sources):
                there = held.at[flip, pl.ds(s * rows, rows)]
                copies.append(pltpu.make_async_copy(source_ref, there, sems.at[flip, s]))
        for copy in copies:
            copy.start()
        to = lax.broadcasted_iota(jnp.int32, (total, total), 0)
        source = lax.broadcasted_iota(jnp.int32, (total, total), 1)
        slot = source // rows
        move = jnp.where(slot == 1, outer - 1, jnp.where(slot == 2, 1, jnp.where(slot == 3, 2, 0)))
        at_x = (at_ref[0] + move) % outer
        at_z = source % rows // (high * own)
        at_high = source % (high * own) // own
        goes = at_z * inner + (at_high * outer + at_x) * own + source % own
        pick = jnp.where(to == goes, 1.0, 0.0).astype(jnp.bfloat16)
        for copy in copies:
            copy.wait()
        for flip in range(flips):
            moved = jnp.dot(pick, held[flip], preferred_element_type=jnp.float32)
            where = (at_ref[1] + flip) % flips
            out_ref[:, pl.ds(where, 1)] = moved.astype(jnp.bfloat16).reshape((deep, 1, inner, width))

    hbm = pl.BlockSpec(memory_space=pltpu.HBM)
    return pl.pallas_call(
        kernel,
        in_specs=[pl.BlockSpec(memory_space=pltpu.SMEM)] + [hbm] * 5,
        out_specs=VMEM,
        out_shape=jax.ShapeDtypeStruct((deep, flips, inner, width), jnp.bfloat16),
        scratch_shapes=[
            pltpu.VMEM((flips, total, width), jnp.bfloat16),
            pltpu.SemaphoreType.DMA((flips, outer)),
        ],
        compiler_params=pltpu.CompilerParams(vmem_limit_bytes=60 * 2**20),
        cost_estimate=pl.CostEstimate(
            flops=6 * flips * total * total * width,
            bytes_accessed=4 * flips * total * width,
            transcendentals=0,
        ),
    )(place_of, pair, before, after, *far)


def score(place_of, own_core, other_core, stored):
    deep, flips, inner, width = own_core.shape
    capacity = stored.shape[0]
    blocks = deep * flips
    half, wide = blocks // 2, capacity // 2

    def kernel(at_ref, own_ref, other_ref, stored_ref, out_ref, held, kept, sems):
        i = pl.program_id(0)
        queries = [
            pltpu.make_async_copy(
                (own_ref, other_ref)[j // 2].at[pl.ds(j % 2 * half, half)], held.at[j], sems.at[j]
            )
            for j in range(4)
        ]
        columns = [
            pltpu.make_async_copy(stored_ref.at[pl.ds(h * wide, wide)], kept.at[h], sems.at[4 + h])
            for h in range(2)
        ]

        @pl.when(i == 0)
        def _():
            for copy in (queries[0], columns[0], columns[1], *queries[1:]):
                copy.start()

        for j in range(4):
            for h in range(2):

                @pl.when(i == 2 * j + h)
                def _():
                    if h == 0:
                        queries[j].wait()
                    if j == 0:
                        columns[h].wait()
                    scores = lax.dot_general(
                        held[j].reshape((half * inner, width)),
                        kept[h],
                        (((1,), (1,)), ((), ())),
                        preferred_element_type=jnp.float32,
                    )
                    scores = scores.astype(jnp.bfloat16).reshape((half, 1, inner, wide))
                    out_ref[:, :, :, h * wide : (h + 1) * wide] = scores

    hbm = pl.BlockSpec(memory_space=pltpu.HBM)
    out = pl.pallas_call(
        kernel,
        grid_spec=pltpu.PrefetchScalarGridSpec(
            num_scalar_prefetch=1,
            grid=(8,),
            in_specs=[hbm, hbm, hbm],
            out_specs=pl.BlockSpec(
                (half, 1, inner, capacity), lambda i, at: (i // 2 % 2, (at[2] + i // 4) % 2, 0, 0)
            ),
            scratch_shapes=[
                pltpu.VMEM((4, half, inner, width), jnp.bfloat16),
                pltpu.VMEM((2, wide, width), jnp.bfloat16),
                pltpu.SemaphoreType.DMA((6,)),
            ],
        ),
        out_shape=jax.ShapeDtypeStruct((blocks, 2, inner, capacity), jnp.bfloat16),
        compiler_params=pltpu.CompilerParams(vmem_limit_bytes=60 * 2**20),
        cost_estimate=pl.CostEstimate(
            flops=4 * blocks * inner * capacity * width,
            bytes_accessed=12 * 2**20,
            transcendentals=0,
        ),
    )(place_of, *(a.reshape((blocks, inner, width)) for a in (own_core, other_core)), stored)
    return out.reshape((-1, capacity))


def body(gradients, destinations, queries, left_factor, right_factor):
    owners = lax.axis_size(STORE)
    rows, width = gradients.shape
    bucket = 2 * rows // owners
    capacity = owners * bucket
    own = queries.shape[0]
    order = (lax.axis_size("z"), lax.axis_size("y_hi"), own)

    line = gather(queries.reshape((-1, 128)), ("z", "y_hi"))
    buffer = prepare(gradients, destinations[None], left_factor, right_factor, bucket, capacity)
    line, buffer = lax.optimization_barrier((line, buffer))
    near = shift(line, "y_lo", 1)
    stored = exchange(buffer.reshape((owners, bucket, width)), STORE).reshape((capacity, width))

    pair = jnp.stack([line, near]).reshape((2, -1, width))
    before, after = shift(pair, "x", 1), shift(pair, "x", -1)
    far = (shift(before[0], "x", 1), shift(after[1], "x", -1))
    place_of = jnp.stack([lax.axis_index(a) for a in ("x", "y_lo", "core")]).astype(jnp.int32)
    mine = reorder(place_of, pair, before, after, far, order)
    others = shift(mine, "core", 1)
    return score(place_of, mine, others, stored)


def solution(mesh):
    fine = Mesh(mesh.devices.reshape((8, 2, 2, 4, 4)), STORE + PROD)
    whole = STORE + PROD
    return jax.shard_map(
        body,
        mesh=fine,
        in_specs=(P(whole, None), P(whole), P(whole, None), P(), P()),
        out_specs=P(None, whole),
        check_vma=False,
    )
```

```python
import math

import jax
import jax.numpy as jnp
from jax import lax
from jax.experimental import pallas as pl
from jax.experimental.pallas import tpu as pltpu
from jax.sharding import Mesh, PartitionSpec as P

STORE = ("z", "y_lo", "core")
PROD = ("y_two", "y_one", "x")
VMEM = pl.BlockSpec(memory_space=pltpu.VMEM)


def exchange(block, axis):
    return lax.all_to_all(block, axis, split_axis=0, concat_axis=0, tiled=True)


def gather(block, axis):
    count = lax.axis_size(axis)
    return exchange(jnp.broadcast_to(block[None], (count,) + block.shape), axis)


def shift(block, axis, by):
    count = lax.axis_size(axis)
    return lax.ppermute(block, axis, [(i, (i + by) % count) for i in range(count)])


def slots_of(targets, bucket):
    rows = targets.shape[1]
    above = lax.broadcasted_iota(jnp.int32, (rows, rows), 0)
    along = lax.broadcasted_iota(jnp.int32, (rows, rows), 1)
    upright = jnp.sum(jnp.where(above == along, targets, 0), axis=1, keepdims=True)
    earlier = jnp.where((upright == targets) & (above < along), 1, 0)
    return targets * bucket + jnp.sum(earlier, axis=0, keepdims=True)


def prepare(gradients, targets, left, right, bucket, capacity, step=1024):
    rows, width = gradients.shape
    deep, fine = left.shape[1], right.shape[0]
    steps = width // step

    def kernel(targets_ref, rows_ref, left_ref, right_ref, out_ref, product, squares, pick):
        i = pl.program_id(0)

        @pl.when(i == 0)
        def _():
            tiled = jnp.concatenate([right_ref[...]] * (step // fine), axis=1)
            above = lax.broadcasted_iota(jnp.int32, (deep, step), 0)
            along = lax.broadcasted_iota(jnp.int32, (deep, step), 1)
            total = jnp.zeros((rows, 1), jnp.float32)
            for j in range(steps):
                spread = lax.dot_general(
                    left_ref[...],
                    jnp.where(above == j * (step // fine) + along // fine, 1.0, 0.0),
                    (((0,), (0,)), ((), ())),
                    preferred_element_type=jnp.float32,
                    precision=lax.Precision.HIGHEST,
                )
                factor = (spread[:, None, :] * tiled[None]).reshape((width, step))
                high = factor.astype(jnp.bfloat16)
                low = (factor - high.astype(jnp.float32)).astype(jnp.bfloat16)
                part = jnp.dot(rows_ref[...], high, preferred_element_type=jnp.float32)
                part = part + jnp.dot(rows_ref[...], low, preferred_element_type=jnp.float32)
                product[j] = part
                total = total + jnp.sum(part * part, axis=1, keepdims=True)
            squares[...] = lax.rsqrt(total / width + 1e-06) * (1.0 / math.sqrt(width))
            slots = slots_of(targets_ref[...], bucket)
            at = lax.broadcasted_iota(jnp.int32, (capacity, rows), 0)
            pick[...] = jnp.where(at == slots, 1.0, 0.0).astype(jnp.bfloat16)

        @pl.when(i > 0)
        def _():
            normal = (product[i - 1] * squares[...]).astype(jnp.bfloat16)
            out_ref[...] = jnp.dot(
                pick[...], normal, preferred_element_type=jnp.float32
            ).astype(jnp.bfloat16)

    return pl.pallas_call(
        kernel,
        grid=(steps + 1,),
        in_specs=[
            pl.BlockSpec((1, rows), lambda i: (0, 0)),
            pl.BlockSpec((rows, width), lambda i: (0, 0)),
            pl.BlockSpec((deep, deep), lambda i: (0, 0)),
            pl.BlockSpec((fine, fine), lambda i: (0, 0)),
        ],
        out_specs=pl.BlockSpec((capacity, step), lambda i: (0, jnp.maximum(i - 1, 0))),
        out_shape=jax.ShapeDtypeStruct((capacity, width), jnp.bfloat16),
        scratch_shapes=[
            pltpu.VMEM((steps, rows, step), jnp.float32),
            pltpu.VMEM((rows, 1), jnp.float32),
            pltpu.VMEM((capacity, rows), jnp.bfloat16),
        ],
        compiler_params=pltpu.CompilerParams(vmem_limit_bytes=60 * 2**20),
        cost_estimate=pl.CostEstimate(
            flops=2 * rows * width * (2 * width + capacity),
            bytes_accessed=6 * 2**20,
            transcendentals=0,
        ),
    )(targets, gradients, left, right)


def reorder(place_of, pair, before, after, far, order):
    deep, high, own = order
    flips, rows, width = pair.shape
    outer = lax.axis_size("x")
    inner = high * outer * own
    total = outer * rows

    def kernel(at_ref, pair_ref, before_ref, after_ref, far0_ref, far1_ref, out_ref, held, sems):
        copies = []
        for flip, far_ref in enumerate((far0_ref, far1_ref)):
            sources = [ref.at[flip] for ref in (pair_ref, before_ref, after_ref)] + [far_ref]
            for s, source_ref in enumerate(sources):
                there = held.at[flip, pl.ds(s * rows, rows)]
                copies.append(pltpu.make_async_copy(source_ref, there, sems.at[flip, s]))
        for copy in copies:
            copy.start()
        to = lax.broadcasted_iota(jnp.int32, (total, total), 0)
        source = lax.broadcasted_iota(jnp.int32, (total, total), 1)
        slot = source // rows
        move = jnp.where(slot == 1, outer - 1, jnp.where(slot == 2, 1, jnp.where(slot == 3, 2, 0)))
        at_x = (at_ref[0] + move) % outer
        at_z = source % rows // (high * own)
        at_high = (source % (high * own) // own) ^ at_ref[3]
        goes = at_z * inner + (at_high * outer + at_x) * own + source % own
        pick = jnp.where(to == goes, 1.0, 0.0).astype(jnp.bfloat16)
        for copy in copies:
            copy.wait()
        for flip in range(flips):
            moved = jnp.dot(pick, held[flip], preferred_element_type=jnp.float32)
            where = (at_ref[1] + flip) % flips
            out_ref[:, pl.ds(where, 1)] = moved.astype(jnp.bfloat16).reshape((deep, 1, inner, width))

    hbm = pl.BlockSpec(memory_space=pltpu.HBM)
    return pl.pallas_call(
        kernel,
        in_specs=[pl.BlockSpec(memory_space=pltpu.SMEM)] + [hbm] * 5,
        out_specs=VMEM,
        out_shape=jax.ShapeDtypeStruct((deep, flips, inner, width), jnp.bfloat16),
        scratch_shapes=[
            pltpu.VMEM((flips, total, width), jnp.bfloat16),
            pltpu.SemaphoreType.DMA((flips, outer)),
        ],
        compiler_params=pltpu.CompilerParams(vmem_limit_bytes=60 * 2**20),
        cost_estimate=pl.CostEstimate(
            flops=6 * flips * total * total * width,
            bytes_accessed=4 * flips * total * width,
            transcendentals=0,
        ),
    )(place_of, pair, before, after, *far)


def score(place_of, own_core, other_core, stored):
    deep, flips, inner, width = own_core.shape
    capacity = stored.shape[0]
    blocks = deep * flips
    half = blocks // 2

    def kernel(at_ref, own_ref, other_ref, stored_ref, out_ref, held, sems):
        i = pl.program_id(0)
        copies = [
            pltpu.make_async_copy(
                (own_ref, other_ref)[j // 2].at[pl.ds(j % 2 * half, half)], held.at[j], sems.at[j]
            )
            for j in range(4)
        ]

        @pl.when(i == 0)
        def _():
            for copy in copies:
                copy.start()

        for j in range(4):

            @pl.when(i == j)
            def _():
                copies[j].wait()
                scores = lax.dot_general(
                    held[j].reshape((half * inner, width)),
                    stored_ref[...],
                    (((1,), (1,)), ((), ())),
                    preferred_element_type=jnp.float32,
                )
                out_ref[...] = scores.astype(jnp.bfloat16).reshape((half, 1, inner, capacity))

    hbm = pl.BlockSpec(memory_space=pltpu.HBM)
    own_core, other_core = (
        pltpu.with_memory_space_constraint(a.reshape((blocks, inner, width)), pltpu.HBM)
        for a in (own_core, other_core)
    )
    out = pl.pallas_call(
        kernel,
        grid_spec=pltpu.PrefetchScalarGridSpec(
            num_scalar_prefetch=1,
            grid=(4,),
            in_specs=[hbm, hbm, VMEM],
            out_specs=pl.BlockSpec(
                (half, 1, inner, capacity), lambda i, at: (i % 2, (at[2] + i // 2) % 2, 0, 0)
            ),
            scratch_shapes=[
                pltpu.VMEM((4, half, inner, width), jnp.bfloat16),
                pltpu.SemaphoreType.DMA((4,)),
            ],
        ),
        out_shape=jax.ShapeDtypeStruct((blocks, 2, inner, capacity), jnp.bfloat16),
        compiler_params=pltpu.CompilerParams(vmem_limit_bytes=24 * 2**20),
        cost_estimate=pl.CostEstimate(
            flops=4 * blocks * inner * capacity * width,
            bytes_accessed=12 * 2**20,
            transcendentals=0,
        ),
    )(place_of, own_core, other_core, stored)
    return out.reshape((-1, capacity))


def body(gradients, destinations, queries, left_factor, right_factor):
    owners = lax.axis_size(STORE)
    rows, width = gradients.shape
    bucket = 2 * rows // owners
    capacity = owners * bucket
    own = queries.shape[0]
    order = (lax.axis_size("z"), lax.axis_size(("y_two", "y_one")), own)

    line = queries.reshape((-1, 128))
    line = gather(jnp.stack([line, shift(line, "y_one", 1)]), ("z", "y_two"))
    buffer = prepare(gradients, destinations[None], left_factor, right_factor, bucket, capacity)
    line, buffer = lax.optimization_barrier((line, buffer))
    near = shift(line, "y_lo", 1)
    stored = exchange(buffer.reshape((owners, bucket, width)), STORE).reshape((capacity, width))

    pair = jnp.stack([line, near]).reshape((2, -1, width))
    before, after = shift(pair, "x", 1), shift(pair, "x", -1)
    far = (shift(before[0], "x", 1), shift(after[1], "x", -1))
    place_of = jnp.stack([lax.axis_index(a) for a in ("x", "y_lo", "core", "y_one")])
    place_of = place_of.astype(jnp.int32)
    mine = reorder(place_of, pair, before, after, far, order)
    others = shift(mine, "core", 1)
    return score(place_of, mine, others, stored)


def solution(mesh):
    fine = Mesh(mesh.devices.reshape((8, 2, 2, 2, 2, 4)), STORE + PROD)
    whole = STORE + PROD
    return jax.shard_map(
        body,
        mesh=fine,
        in_specs=(P(whole, None), P(whole), P(whole, None), P(), P()),
        out_specs=P(None, whole),
        check_vma=False,
    )
```

```python
import math

import jax
import jax.numpy as jnp
from jax import lax
from jax.experimental import pallas as pl
from jax.experimental.pallas import tpu as pltpu
from jax.sharding import Mesh, PartitionSpec as P

STORE = ("z", "y_lo", "core")
PROD = ("y_hi", "x")
VMEM = pl.BlockSpec(memory_space=pltpu.VMEM)


def exchange(block, axis):
    return lax.all_to_all(block, axis, split_axis=0, concat_axis=0, tiled=True)


def gather(block, axis):
    count = lax.axis_size(axis)
    return exchange(jnp.broadcast_to(block[None], (count,) + block.shape), axis)


def shift(block, axis, by):
    count = lax.axis_size(axis)
    return lax.ppermute(block, axis, [(i, (i + by) % count) for i in range(count)])


def slots_of(targets, bucket):
    rows = targets.shape[1]
    above = lax.broadcasted_iota(jnp.int32, (rows, rows), 0)
    along = lax.broadcasted_iota(jnp.int32, (rows, rows), 1)
    upright = jnp.sum(jnp.where(above == along, targets, 0), axis=1, keepdims=True)
    earlier = jnp.where((upright == targets) & (above < along), 1, 0)
    return targets * bucket + jnp.sum(earlier, axis=0, keepdims=True)


def prepare(gradients, targets, left, right, bucket, capacity, step=1024):
    rows, width = gradients.shape
    deep, fine = left.shape[1], right.shape[0]
    steps = width // step

    def kernel(targets_ref, rows_ref, left_ref, right_ref, out_ref, product, squares, pick):
        i = pl.program_id(0)

        @pl.when(i == 0)
        def _():
            tiled = jnp.concatenate([right_ref[...]] * (step // fine), axis=1)
            above = lax.broadcasted_iota(jnp.int32, (deep, step), 0)
            along = lax.broadcasted_iota(jnp.int32, (deep, step), 1)
            total = jnp.zeros((rows, 1), jnp.float32)
            for j in range(steps):
                spread = lax.dot_general(
                    left_ref[...],
                    jnp.where(above == j * (step // fine) + along // fine, 1.0, 0.0),
                    (((0,), (0,)), ((), ())),
                    preferred_element_type=jnp.float32,
                    precision=lax.Precision.HIGHEST,
                )
                factor = (spread[:, None, :] * tiled[None]).reshape((width, step))
                high = factor.astype(jnp.bfloat16)
                low = (factor - high.astype(jnp.float32)).astype(jnp.bfloat16)
                part = jnp.dot(rows_ref[...], high, preferred_element_type=jnp.float32)
                part = part + jnp.dot(rows_ref[...], low, preferred_element_type=jnp.float32)
                product[j] = part
                total = total + jnp.sum(part * part, axis=1, keepdims=True)
            squares[...] = lax.rsqrt(total / width + 1e-06) * (1.0 / math.sqrt(width))
            slots = slots_of(targets_ref[...], bucket)
            at = lax.broadcasted_iota(jnp.int32, (capacity, rows), 0)
            pick[...] = jnp.where(at == slots, 1.0, 0.0).astype(jnp.bfloat16)

        @pl.when(i > 0)
        def _():
            normal = (product[i - 1] * squares[...]).astype(jnp.bfloat16)
            out_ref[...] = jnp.dot(
                pick[...], normal, preferred_element_type=jnp.float32
            ).astype(jnp.bfloat16)

    return pl.pallas_call(
        kernel,
        grid=(steps + 1,),
        in_specs=[
            pl.BlockSpec((1, rows), lambda i: (0, 0)),
            pl.BlockSpec((rows, width), lambda i: (0, 0)),
            pl.BlockSpec((deep, deep), lambda i: (0, 0)),
            pl.BlockSpec((fine, fine), lambda i: (0, 0)),
        ],
        out_specs=pl.BlockSpec((capacity, step), lambda i: (0, jnp.maximum(i - 1, 0))),
        out_shape=jax.ShapeDtypeStruct((capacity, width), jnp.bfloat16),
        scratch_shapes=[
            pltpu.VMEM((steps, rows, step), jnp.float32),
            pltpu.VMEM((rows, 1), jnp.float32),
            pltpu.VMEM((capacity, rows), jnp.bfloat16),
        ],
        compiler_params=pltpu.CompilerParams(vmem_limit_bytes=60 * 2**20),
        cost_estimate=pl.CostEstimate(
            flops=2 * rows * width * (2 * width + capacity),
            bytes_accessed=6 * 2**20,
            transcendentals=0,
        ),
    )(targets, gradients, left, right)


def reorder(place_of, pair, before, after, far, order):
    deep, high, own = order
    flips, rows, width = pair.shape
    outer = lax.axis_size("x")
    inner = high * outer * own
    total = outer * rows

    def kernel(at_ref, pair_ref, before_ref, after_ref, far0_ref, far1_ref, out_ref, held, sems):
        copies = []
        for flip, far_ref in enumerate((far0_ref, far1_ref)):
            sources = [ref.at[flip] for ref in (pair_ref, before_ref, after_ref)] + [far_ref]
            for s, source_ref in enumerate(sources):
                there = held.at[flip, pl.ds(s * rows, rows)]
                copies.append(pltpu.make_async_copy(source_ref, there, sems.at[flip, s]))
        for copy in copies:
            copy.start()
        to = lax.broadcasted_iota(jnp.int32, (total, total), 0)
        source = lax.broadcasted_iota(jnp.int32, (total, total), 1)
        slot = source // rows
        move = jnp.where(slot == 1, outer - 1, jnp.where(slot == 2, 1, jnp.where(slot == 3, 2, 0)))
        at_x = (at_ref[0] + move) % outer
        at_z = source % rows // (high * own)
        at_high = source % (high * own) // own
        goes = at_z * inner + (at_high * outer + at_x) * own + source % own
        pick = jnp.where(to == goes, 1.0, 0.0).astype(jnp.bfloat16)
        for copy in copies:
            copy.wait()
        for flip in range(flips):
            moved = jnp.dot(pick, held[flip], preferred_element_type=jnp.float32)
            where = (at_ref[1] + flip) % flips
            out_ref[:, pl.ds(where, 1)] = moved.astype(jnp.bfloat16).reshape((deep, 1, inner, width))

    hbm = pl.BlockSpec(memory_space=pltpu.HBM)
    return pl.pallas_call(
        kernel,
        in_specs=[pl.BlockSpec(memory_space=pltpu.SMEM)] + [hbm] * 5,
        out_specs=VMEM,
        out_shape=jax.ShapeDtypeStruct((deep, flips, inner, width), jnp.bfloat16),
        scratch_shapes=[
            pltpu.VMEM((flips, total, width), jnp.bfloat16),
            pltpu.SemaphoreType.DMA((flips, outer)),
        ],
        compiler_params=pltpu.CompilerParams(vmem_limit_bytes=60 * 2**20),
        cost_estimate=pl.CostEstimate(
            flops=6 * flips * total * total * width,
            bytes_accessed=4 * flips * total * width,
            transcendentals=0,
        ),
    )(place_of, pair, before, after, *far)


def score(place_of, own_core, other_core, stored):
    deep, flips, inner, width = own_core.shape
    capacity = stored.shape[0]
    blocks = deep * flips
    half = blocks // 2

    def kernel(at_ref, own_ref, other_ref, stored_ref, out_ref, held, sems):
        i = pl.program_id(0)
        copies = [
            pltpu.make_async_copy(
                (own_ref, other_ref)[j // 2].at[pl.ds(j % 2 * half, half)], held.at[j], sems.at[j]
            )
            for j in range(4)
        ]

        @pl.when(i == 0)
        def _():
            for copy in copies:
                copy.start()

        for j in range(4):

            @pl.when(i == j)
            def _():
                copies[j].wait()
                scores = lax.dot_general(
                    held[j].reshape((half * inner, width)),
                    stored_ref[...],
                    (((1,), (1,)), ((), ())),
                    preferred_element_type=jnp.float32,
                )
                out_ref[...] = scores.astype(jnp.bfloat16).reshape((half, 1, inner, capacity))

    hbm = pl.BlockSpec(memory_space=pltpu.HBM)
    own_core, other_core = (
        pltpu.with_memory_space_constraint(a.reshape((blocks, inner, width)), pltpu.HBM)
        for a in (own_core, other_core)
    )
    out = pl.pallas_call(
        kernel,
        grid_spec=pltpu.PrefetchScalarGridSpec(
            num_scalar_prefetch=1,
            grid=(4,),
            in_specs=[hbm, hbm, VMEM],
            out_specs=pl.BlockSpec(
                (half, 1, inner, capacity), lambda i, at: (i % 2, (at[2] + i // 2) % 2, 0, 0)
            ),
            scratch_shapes=[
                pltpu.VMEM((4, half, inner, width), jnp.bfloat16),
                pltpu.SemaphoreType.DMA((4,)),
            ],
        ),
        out_shape=jax.ShapeDtypeStruct((blocks, 2, inner, capacity), jnp.bfloat16),
        compiler_params=pltpu.CompilerParams(vmem_limit_bytes=24 * 2**20),
        cost_estimate=pl.CostEstimate(
            flops=4 * blocks * inner * capacity * width,
            bytes_accessed=12 * 2**20,
            transcendentals=0,
        ),
    )(place_of, own_core, other_core, stored)
    return out.reshape((-1, capacity))


def body(gradients, destinations, queries, left_factor, right_factor):
    owners = lax.axis_size(STORE)
    rows, width = gradients.shape
    bucket = 2 * rows // owners
    capacity = owners * bucket
    own = queries.shape[0]
    order = (lax.axis_size("z"), lax.axis_size("y_hi"), own)

    line = gather(queries.reshape((-1, 128)), ("z", "y_hi"))
    buffer = prepare(gradients, destinations[None], left_factor, right_factor, bucket, capacity)
    line, buffer = lax.optimization_barrier((line, buffer))
    near = shift(line, "y_lo", 1)
    stored = exchange(buffer.reshape((owners, bucket, width)), STORE).reshape((capacity, width))

    pair = jnp.stack([line, near]).reshape((2, -1, width))
    before, after = shift(pair, "x", 1), shift(pair, "x", -1)
    far = (shift(before[0], "x", 1), shift(after[1], "x", -1))
    place_of = jnp.stack([lax.axis_index(a) for a in ("x", "y_lo", "core")]).astype(jnp.int32)
    mine = reorder(place_of, pair, before, after, far, order)
    others = shift(mine, "core", 1)
    return score(place_of, mine, others, stored)


def solution(mesh):
    fine = Mesh(mesh.devices.reshape((8, 2, 2, 4, 4)), STORE + PROD)
    whole = STORE + PROD
    return jax.shard_map(
        body,
        mesh=fine,
        in_specs=(P(whole, None), P(whole), P(whole, None), P(), P()),
        out_specs=P(None, whole),
        check_vma=False,
    )
```

```python
import math

import jax
import jax.numpy as jnp
from jax import lax
from jax.experimental import pallas as pl
from jax.experimental.pallas import tpu as pltpu
from jax.sharding import Mesh, PartitionSpec as P

STORE = ("z", "y_lo", "core")
PROD = ("y_hi", "x")
VMEM = pl.BlockSpec(memory_space=pltpu.VMEM)


def exchange(block, axis):
    return lax.all_to_all(block, axis, split_axis=0, concat_axis=0, tiled=True)


def gather(block, axis):
    count = lax.axis_size(axis)
    return exchange(jnp.broadcast_to(block[None], (count,) + block.shape), axis)


def shift(block, axis, by):
    count = lax.axis_size(axis)
    return lax.ppermute(block, axis, [(i, (i + by) % count) for i in range(count)])


def slots_of(targets, bucket):
    rows = targets.shape[1]
    above = lax.broadcasted_iota(jnp.int32, (rows, rows), 0)
    along = lax.broadcasted_iota(jnp.int32, (rows, rows), 1)
    upright = jnp.sum(jnp.where(above == along, targets, 0), axis=1, keepdims=True)
    earlier = jnp.where((upright == targets) & (above < along), 1, 0)
    return targets * bucket + jnp.sum(earlier, axis=0, keepdims=True)


def prepare(gradients, targets, left, right, bucket, capacity, step=1024):
    rows, width = gradients.shape
    deep, fine = left.shape[1], right.shape[0]
    steps = width // step

    def kernel(targets_ref, rows_ref, left_ref, right_ref, out_ref, product, squares, pick):
        i = pl.program_id(0)

        @pl.when(i == 0)
        def _():
            tiled = jnp.concatenate([right_ref[...]] * (step // fine), axis=1)
            above = lax.broadcasted_iota(jnp.int32, (deep, step), 0)
            along = lax.broadcasted_iota(jnp.int32, (deep, step), 1)
            total = jnp.zeros((rows, 1), jnp.float32)
            for j in range(steps):
                spread = lax.dot_general(
                    left_ref[...],
                    jnp.where(above == j * (step // fine) + along // fine, 1.0, 0.0),
                    (((0,), (0,)), ((), ())),
                    preferred_element_type=jnp.float32,
                    precision=lax.Precision.HIGHEST,
                )
                factor = (spread[:, None, :] * tiled[None]).reshape((width, step))
                high = factor.astype(jnp.bfloat16)
                low = (factor - high.astype(jnp.float32)).astype(jnp.bfloat16)
                part = jnp.dot(rows_ref[...], high, preferred_element_type=jnp.float32)
                part = part + jnp.dot(rows_ref[...], low, preferred_element_type=jnp.float32)
                product[j] = part
                total = total + jnp.sum(part * part, axis=1, keepdims=True)
            squares[...] = lax.rsqrt(total / width + 1e-06) * (1.0 / math.sqrt(width))
            slots = slots_of(targets_ref[...], bucket)
            at = lax.broadcasted_iota(jnp.int32, (capacity, rows), 0)
            pick[...] = jnp.where(at == slots, 1.0, 0.0).astype(jnp.bfloat16)

        @pl.when(i > 0)
        def _():
            normal = (product[i - 1] * squares[...]).astype(jnp.bfloat16)
            out_ref[...] = jnp.dot(
                pick[...], normal, preferred_element_type=jnp.float32
            ).astype(jnp.bfloat16)

    return pl.pallas_call(
        kernel,
        grid=(steps + 1,),
        in_specs=[
            pl.BlockSpec((1, rows), lambda i: (0, 0)),
            pl.BlockSpec((rows, width), lambda i: (0, 0)),
            pl.BlockSpec((deep, deep), lambda i: (0, 0)),
            pl.BlockSpec((fine, fine), lambda i: (0, 0)),
        ],
        out_specs=pl.BlockSpec((capacity, step), lambda i: (0, jnp.maximum(i - 1, 0))),
        out_shape=jax.ShapeDtypeStruct((capacity, width), jnp.bfloat16),
        scratch_shapes=[
            pltpu.VMEM((steps, rows, step), jnp.float32),
            pltpu.VMEM((rows, 1), jnp.float32),
            pltpu.VMEM((capacity, rows), jnp.bfloat16),
        ],
        compiler_params=pltpu.CompilerParams(vmem_limit_bytes=60 * 2**20),
        cost_estimate=pl.CostEstimate(
            flops=2 * rows * width * (2 * width + capacity),
            bytes_accessed=6 * 2**20,
            transcendentals=0,
        ),
    )(targets, gradients, left, right)


def reorder(place_of, pair, before, after, far, order):
    deep, high, own = order
    flips, rows, width = pair.shape
    outer = lax.axis_size("x")
    inner = high * outer * own
    total = outer * rows

    def kernel(at_ref, pair_ref, before_ref, after_ref, far0_ref, far1_ref, out_ref, held, sems):
        copies = []
        for flip, far_ref in enumerate((far0_ref, far1_ref)):
            sources = [ref.at[flip] for ref in (pair_ref, before_ref, after_ref)] + [far_ref]
            for s, source_ref in enumerate(sources):
                there = held.at[flip, pl.ds(s * rows, rows)]
                copies.append(pltpu.make_async_copy(source_ref, there, sems.at[flip, s]))
        for copy in copies:
            copy.start()
        to = lax.broadcasted_iota(jnp.int32, (total, total), 0)
        source = lax.broadcasted_iota(jnp.int32, (total, total), 1)
        slot = source // rows
        move = jnp.where(slot == 1, outer - 1, jnp.where(slot == 2, 1, jnp.where(slot == 3, 2, 0)))
        at_x = (at_ref[0] + move) % outer
        at_high = source % rows // (deep * own)
        at_z = source % (deep * own) // own
        goes = at_z * inner + (at_high * outer + at_x) * own + source % own
        pick = jnp.where(to == goes, 1.0, 0.0).astype(jnp.bfloat16)
        for copy in copies:
            copy.wait()
        for flip in range(flips):
            moved = jnp.dot(pick, held[flip], preferred_element_type=jnp.float32)
            where = (at_ref[1] + flip) % flips
            out_ref[:, pl.ds(where, 1)] = moved.astype(jnp.bfloat16).reshape((deep, 1, inner, width))

    hbm = pl.BlockSpec(memory_space=pltpu.HBM)
    return pl.pallas_call(
        kernel,
        in_specs=[pl.BlockSpec(memory_space=pltpu.SMEM)] + [hbm] * 5,
        out_specs=VMEM,
        out_shape=jax.ShapeDtypeStruct((deep, flips, inner, width), jnp.bfloat16),
        scratch_shapes=[
            pltpu.VMEM((flips, total, width), jnp.bfloat16),
            pltpu.SemaphoreType.DMA((flips, outer)),
        ],
        compiler_params=pltpu.CompilerParams(vmem_limit_bytes=60 * 2**20),
        cost_estimate=pl.CostEstimate(
            flops=6 * flips * total * total * width,
            bytes_accessed=4 * flips * total * width,
            transcendentals=0,
        ),
    )(place_of, pair, before, after, *far)


def score(place_of, own_core, other_core, stored):
    deep, flips, inner, width = own_core.shape
    capacity = stored.shape[0]
    blocks = deep * flips
    half = blocks // 2

    def kernel(at_ref, own_ref, other_ref, stored_ref, out_ref, held, sems):
        i = pl.program_id(0)
        copies = [
            pltpu.make_async_copy(
                (own_ref, other_ref)[j // 2].at[pl.ds(j % 2 * half, half)], held.at[j], sems.at[j]
            )
            for j in range(4)
        ]

        @pl.when(i == 0)
        def _():
            for copy in copies:
                copy.start()

        for j in range(4):

            @pl.when(i == j)
            def _():
                copies[j].wait()
                scores = lax.dot_general(
                    held[j].reshape((half * inner, width)),
                    stored_ref[...],
                    (((1,), (1,)), ((), ())),
                    preferred_element_type=jnp.float32,
                )
                out_ref[...] = scores.astype(jnp.bfloat16).reshape((half, 1, inner, capacity))

    hbm = pl.BlockSpec(memory_space=pltpu.HBM)
    own_core, other_core = (
        pltpu.with_memory_space_constraint(a.reshape((blocks, inner, width)), pltpu.HBM)
        for a in (own_core, other_core)
    )
    out = pl.pallas_call(
        kernel,
        grid_spec=pltpu.PrefetchScalarGridSpec(
            num_scalar_prefetch=1,
            grid=(4,),
            in_specs=[hbm, hbm, VMEM],
            out_specs=pl.BlockSpec(
                (half, 1, inner, capacity), lambda i, at: (i % 2, (at[2] + i // 2) % 2, 0, 0)
            ),
            scratch_shapes=[
                pltpu.VMEM((4, half, inner, width), jnp.bfloat16),
                pltpu.SemaphoreType.DMA((4,)),
            ],
        ),
        out_shape=jax.ShapeDtypeStruct((blocks, 2, inner, capacity), jnp.bfloat16),
        compiler_params=pltpu.CompilerParams(vmem_limit_bytes=24 * 2**20),
        cost_estimate=pl.CostEstimate(
            flops=4 * blocks * inner * capacity * width,
            bytes_accessed=12 * 2**20,
            transcendentals=0,
        ),
    )(place_of, own_core, other_core, stored)
    return out.reshape((-1, capacity))


def body(gradients, destinations, queries, left_factor, right_factor):
    owners = lax.axis_size(STORE)
    rows, width = gradients.shape
    bucket = 2 * rows // owners
    capacity = owners * bucket
    own = queries.shape[0]
    order = (lax.axis_size("z"), lax.axis_size("y_hi"), own)

    line = gather(queries.reshape((-1, 128)), ("y_hi", "z"))
    buffer = prepare(gradients, destinations[None], left_factor, right_factor, bucket, capacity)
    line, buffer = lax.optimization_barrier((line, buffer))
    near = shift(line, "y_lo", 1)
    stored = exchange(buffer.reshape((owners, bucket, width)), STORE).reshape((capacity, width))

    pair = jnp.stack([line, near]).reshape((2, -1, width))
    before, after = shift(pair, "x", 1), shift(pair, "x", -1)
    far = (shift(before[0], "x", 1), shift(after[1], "x", -1))
    place_of = jnp.stack([lax.axis_index(a) for a in ("x", "y_lo", "core")]).astype(jnp.int32)
    mine = reorder(place_of, pair, before, after, far, order)
    others = shift(mine, "core", 1)
    return score(place_of, mine, others, stored)


def solution(mesh):
    fine = Mesh(mesh.devices.reshape((8, 2, 2, 4, 4)), STORE + PROD)
    whole = STORE + PROD
    return jax.shard_map(
        body,
        mesh=fine,
        in_specs=(P(whole, None), P(whole), P(whole, None), P(), P()),
        out_specs=P(None, whole),
        check_vma=False,
    )
```

```python
import math

import jax
import jax.numpy as jnp
from jax import lax
from jax.experimental import pallas as pl
from jax.experimental.pallas import tpu as pltpu
from jax.sharding import Mesh, PartitionSpec as P

STORE = ("z", "y_lo", "core")
PROD = ("y_hi", "x")
VMEM = pl.BlockSpec(memory_space=pltpu.VMEM)


def exchange(block, axis):
    return lax.all_to_all(block, axis, split_axis=0, concat_axis=0, tiled=True)


def copies_of(queries, count):
    own, width = queries.shape
    tall = own * width // 128

    def kernel(in_ref, out_ref):
        whole = in_ref[...].astype(jnp.float32)
        parts = [whole[q : q + 1, c : c + 128] for q in range(own) for c in range(0, width, 128)]
        block = jnp.concatenate(parts, axis=0).astype(jnp.bfloat16)
        out_ref[...] = jnp.broadcast_to(block[None], (count, tall, 128))

    return pl.pallas_call(
        kernel, out_shape=jax.ShapeDtypeStruct((count, tall, 128), jnp.bfloat16)
    )(queries)


def shift(block, axis, by):
    count = lax.axis_size(axis)
    return lax.ppermute(block, axis, [(i, (i + by) % count) for i in range(count)])


def slots_of(targets, bucket):
    rows = targets.shape[1]
    above = lax.broadcasted_iota(jnp.int32, (rows, rows), 0)
    along = lax.broadcasted_iota(jnp.int32, (rows, rows), 1)
    upright = jnp.sum(jnp.where(above == along, targets, 0), axis=1, keepdims=True)
    earlier = jnp.where((upright == targets) & (above < along), 1, 0)
    return targets * bucket + jnp.sum(earlier, axis=0, keepdims=True)


def prepare(gradients, targets, left, right, bucket, capacity, step=1024):
    rows, width = gradients.shape
    deep, fine = left.shape[1], right.shape[0]
    steps = width // step

    def kernel(targets_ref, rows_ref, left_ref, right_ref, out_ref, product, squares, pick):
        i = pl.program_id(0)

        @pl.when(i == 0)
        def _():
            tiled = jnp.concatenate([right_ref[...]] * (step // fine), axis=1)
            above = lax.broadcasted_iota(jnp.int32, (deep, step), 0)
            along = lax.broadcasted_iota(jnp.int32, (deep, step), 1)
            total = jnp.zeros((rows, 1), jnp.float32)
            for j in range(steps):
                spread = lax.dot_general(
                    left_ref[...],
                    jnp.where(above == j * (step // fine) + along // fine, 1.0, 0.0),
                    (((0,), (0,)), ((), ())),
                    preferred_element_type=jnp.float32,
                    precision=lax.Precision.HIGHEST,
                )
                factor = (spread[:, None, :] * tiled[None]).reshape((width, step))
                high = factor.astype(jnp.bfloat16)
                low = (factor - high.astype(jnp.float32)).astype(jnp.bfloat16)
                part = jnp.dot(rows_ref[...], high, preferred_element_type=jnp.float32)
                part = part + jnp.dot(rows_ref[...], low, preferred_element_type=jnp.float32)
                product[j] = part
                total = total + jnp.sum(part * part, axis=1, keepdims=True)
            squares[...] = lax.rsqrt(total / width + 1e-06) * (1.0 / math.sqrt(width))
            slots = slots_of(targets_ref[...], bucket)
            at = lax.broadcasted_iota(jnp.int32, (capacity, rows), 0)
            pick[...] = jnp.where(at == slots, 1.0, 0.0).astype(jnp.bfloat16)

        @pl.when(i > 0)
        def _():
            normal = (product[i - 1] * squares[...]).astype(jnp.bfloat16)
            out_ref[...] = jnp.dot(
                pick[...], normal, preferred_element_type=jnp.float32
            ).astype(jnp.bfloat16)

    return pl.pallas_call(
        kernel,
        grid=(steps + 1,),
        in_specs=[
            pl.BlockSpec((1, rows), lambda i: (0, 0)),
            pl.BlockSpec((rows, width), lambda i: (0, 0)),
            pl.BlockSpec((deep, deep), lambda i: (0, 0)),
            pl.BlockSpec((fine, fine), lambda i: (0, 0)),
        ],
        out_specs=pl.BlockSpec((capacity, step), lambda i: (0, jnp.maximum(i - 1, 0))),
        out_shape=jax.ShapeDtypeStruct((capacity, width), jnp.bfloat16),
        scratch_shapes=[
            pltpu.VMEM((steps, rows, step), jnp.float32),
            pltpu.VMEM((rows, 1), jnp.float32),
            pltpu.VMEM((capacity, rows), jnp.bfloat16),
        ],
        compiler_params=pltpu.CompilerParams(vmem_limit_bytes=60 * 2**20),
        cost_estimate=pl.CostEstimate(
            flops=2 * rows * width * (2 * width + capacity),
            bytes_accessed=6 * 2**20,
            transcendentals=0,
        ),
    )(targets, gradients, left, right)


def reorder(place_of, pair, before, after, far, order):
    deep, high, own = order
    flips, rows, width = pair.shape
    outer = lax.axis_size("x")
    inner = high * outer * own
    total = outer * rows

    def kernel(at_ref, pair_ref, before_ref, after_ref, far0_ref, far1_ref, out_ref, held, sems):
        copies = []
        for flip, far_ref in enumerate((far0_ref, far1_ref)):
            sources = [ref.at[flip] for ref in (pair_ref, before_ref, after_ref)] + [far_ref]
            for s, source_ref in enumerate(sources):
                there = held.at[flip, pl.ds(s * rows, rows)]
                copies.append(pltpu.make_async_copy(source_ref, there, sems.at[flip, s]))
        for copy in copies:
            copy.start()
        to = lax.broadcasted_iota(jnp.int32, (total, total), 0)
        source = lax.broadcasted_iota(jnp.int32, (total, total), 1)
        slot = source // rows
        move = jnp.where(slot == 1, outer - 1, jnp.where(slot == 2, 1, jnp.where(slot == 3, 2, 0)))
        at_x = (at_ref[0] + move) % outer
        at_z = source % rows // (high * own)
        at_high = source % (high * own) // own
        goes = at_z * inner + (at_high * outer + at_x) * own + source % own
        pick = jnp.where(to == goes, 1.0, 0.0).astype(jnp.bfloat16)
        for copy in copies:
            copy.wait()
        for flip in range(flips):
            moved = jnp.dot(pick, held[flip], preferred_element_type=jnp.float32)
            where = (at_ref[1] + flip) % flips
            out_ref[:, pl.ds(where, 1)] = moved.astype(jnp.bfloat16).reshape((deep, 1, inner, width))

    hbm = pl.BlockSpec(memory_space=pltpu.HBM)
    return pl.pallas_call(
        kernel,
        in_specs=[pl.BlockSpec(memory_space=pltpu.SMEM)] + [hbm] * 5,
        out_specs=VMEM,
        out_shape=jax.ShapeDtypeStruct((deep, flips, inner, width), jnp.bfloat16),
        scratch_shapes=[
            pltpu.VMEM((flips, total, width), jnp.bfloat16),
            pltpu.SemaphoreType.DMA((flips, outer)),
        ],
        compiler_params=pltpu.CompilerParams(vmem_limit_bytes=60 * 2**20),
        cost_estimate=pl.CostEstimate(
            flops=6 * flips * total * total * width,
            bytes_accessed=4 * flips * total * width,
            transcendentals=0,
        ),
    )(place_of, pair, before, after, *far)


def score(place_of, own_core, other_core, stored):
    deep, flips, inner, width = own_core.shape
    capacity = stored.shape[0]
    blocks = deep * flips
    half = blocks // 2

    def kernel(at_ref, own_ref, other_ref, stored_ref, out_ref, held, sems):
        i = pl.program_id(0)
        copies = [
            pltpu.make_async_copy(
                (own_ref, other_ref)[j // 2].at[pl.ds(j % 2 * half, half)], held.at[j], sems.at[j]
            )
            for j in range(4)
        ]

        @pl.when(i == 0)
        def _():
            for copy in copies:
                copy.start()

        for j in range(4):

            @pl.when(i == j)
            def _():
                copies[j].wait()
                scores = lax.dot_general(
                    held[j].reshape((half * inner, width)),
                    stored_ref[...],
                    (((1,), (1,)), ((), ())),
                    preferred_element_type=jnp.float32,
                )
                out_ref[...] = scores.astype(jnp.bfloat16).reshape((half, 1, inner, capacity))

    hbm = pl.BlockSpec(memory_space=pltpu.HBM)
    own_core, other_core = (
        pltpu.with_memory_space_constraint(a.reshape((blocks, inner, width)), pltpu.HBM)
        for a in (own_core, other_core)
    )
    out = pl.pallas_call(
        kernel,
        grid_spec=pltpu.PrefetchScalarGridSpec(
            num_scalar_prefetch=1,
            grid=(4,),
            in_specs=[hbm, hbm, VMEM],
            out_specs=pl.BlockSpec(
                (half, 1, inner, capacity), lambda i, at: (i % 2, (at[2] + i // 2) % 2, 0, 0)
            ),
            scratch_shapes=[
                pltpu.VMEM((4, half, inner, width), jnp.bfloat16),
                pltpu.SemaphoreType.DMA((4,)),
            ],
        ),
        out_shape=jax.ShapeDtypeStruct((blocks, 2, inner, capacity), jnp.bfloat16),
        compiler_params=pltpu.CompilerParams(vmem_limit_bytes=24 * 2**20),
        cost_estimate=pl.CostEstimate(
            flops=4 * blocks * inner * capacity * width,
            bytes_accessed=12 * 2**20,
            transcendentals=0,
        ),
    )(place_of, own_core, other_core, stored)
    return out.reshape((-1, capacity))


def body(gradients, destinations, queries, left_factor, right_factor):
    owners = lax.axis_size(STORE)
    rows, width = gradients.shape
    bucket = 2 * rows // owners
    capacity = owners * bucket
    own = queries.shape[0]
    order = (lax.axis_size("z"), lax.axis_size("y_hi"), own)

    line = exchange(copies_of(queries, lax.axis_size(("z", "y_hi"))), ("z", "y_hi"))
    buffer = prepare(gradients, destinations[None], left_factor, right_factor, bucket, capacity)
    line, buffer = lax.optimization_barrier((line, buffer))
    near = shift(line, "y_lo", 1)
    stored = exchange(buffer.reshape((owners, bucket, width)), STORE).reshape((capacity, width))

    pair = jnp.stack([line, near]).reshape((2, -1, width))
    before, after = shift(pair, "x", 1), shift(pair, "x", -1)
    far = (shift(before[0], "x", 1), shift(after[1], "x", -1))
    place_of = jnp.stack([lax.axis_index(a) for a in ("x", "y_lo", "core")]).astype(jnp.int32)
    mine = reorder(place_of, pair, before, after, far, order)
    others = shift(mine, "core", 1)
    return score(place_of, mine, others, stored)


def solution(mesh):
    fine = Mesh(mesh.devices.reshape((8, 2, 2, 4, 4)), STORE + PROD)
    whole = STORE + PROD
    return jax.shard_map(
        body,
        mesh=fine,
        in_specs=(P(whole, None), P(whole), P(whole, None), P(), P()),
        out_specs=P(None, whole),
        check_vma=False,
    )
```
